32 devices in a mesh: tiles: 16 (over z, y, core), band: 2 (over x).
Axes of the slice: x: 2, y: 2, z: 4, core: 2. Of those that a mesh axis runs over, the one named last changes fastest.
Arguments:
- optical_depth: bfloat16 [256, 90, 4, 256], P('tiles', None, None, 'band'), may hold values from 0.00049972534 to 0.029907227
- albedo: bfloat16 [256, 90, 256], P('tiles', None, 'band'), may hold values from 0.69921875 to 0.96875
- insolation: bfloat16 [256, 256], P('tiles', 'band'), may hold values from 20 to 100
- sunlit: int32 [256, 2], P('tiles', 'band'), may hold values from 0 to 1, as said below
- point_weight: float32 [4], replicated, may hold values from 0.1 to 1
- anomaly: float32 [256, 90, 256], P('tiles', None, 'band'), may hold values from -6 to 6
Outputs:
- heating: float32 [256, 90, 256], P('tiles', None, 'band')
- smoothed: float32 [256, 90, 256], P('tiles', None, 'band')
The draws below stay inside these ranges and needn't reach their ends.
Inputs may be any that keep to these rules, and one draw needn't show every extreme that they name: In every row, of two blocks that lie half of 2 sectors apart, exactly one is sunlit.
All inputs are finite; a program needn't handle non-finite values.
Results may differ from the reference program's by a relative error of at most 0.00045.
Values may be sent and summed in bfloat16 or wider, within the bound.
A program may use at most 64 MiB of HBM per device.

```python
import math
import jax
import jax.numpy as jnp
from jax import lax

ROWS_DEV = 16
BLOCK = 128
LEV = 90
G = 4
DIFF_STEPS = 4
NROWS = 256
SECTORS = 2
NCOLS = 256


def draw_sunlit(key, part):
    key_start = jax.random.fold_in(key, 11)
    key_flip = jax.random.fold_in(key, 23)
    day_start = jax.random.randint(key_start, (), 0, SECTORS)
    half_sectors = SECTORS // 2
    sector_ids = jnp.arange(half_sectors, dtype=jnp.int32)
    is_day = (sector_ids - day_start) % SECTORS < half_sectors
    flipped = jax.random.randint(key_flip, (NROWS, half_sectors), 0, 8) == 0
    day_first = jnp.logical_xor(is_day[None, :], flipped)
    daylit = jnp.concatenate([day_first, jnp.logical_not(day_first)], axis=1)
    return daylit.astype(jnp.int32)


def level_of(stream_key, dims, cuts, low, top_value):
    gain, own = 1.0, jax.random.fold_in(stream_key, 6)
    for dim, parts in cuts:
        draws = jnp.exp(jax.random.uniform(jax.random.fold_in(own, dim), (parts,), jnp.float32, low / len(cuts), top_value / len(cuts)))
        gain = gain * jnp.repeat(draws, dims[dim] // parts).reshape([-1 if axis == dim else 1 for axis in range(len(dims))])
    return gain


def gaussian(own_key, shape, scale, bound, split=(), kind=jnp.bfloat16):
    level = level_of(own_key, shape, split, -0.22, 0.18) if split else 1.0
    result = jax.random.normal(own_key, shape, jnp.float32) * scale * level
    return jnp.minimum(jnp.maximum(result, -bound), bound).astype(kind)


def setup_inputs(seed: int = 0) -> dict:
    key_list = jax.random.split(jax.random.key(seed), 7)
    optical_depth = jnp.clip(jnp.exp(math.log(0.029907227) - 4.091797 * jax.random.uniform(key_list[0], (NROWS, LEV, G, NCOLS), jnp.float32) ** level_of(key_list[0], (NROWS, LEV, G, NCOLS), ((0, 16), (3, 2)), -0.2, 0.2)), 0.00049972534, 0.029907227).astype(jnp.bfloat16)
    albedo = jnp.clip(0.69921875 + 0.26953125 * jax.random.uniform(key_list[1], (NROWS, LEV, NCOLS), jnp.float32) ** level_of(key_list[1], (NROWS, LEV, NCOLS), ((0, 16), (2, 2)), -0.2, 0.2), 0.69921875, 0.96875).astype(jnp.bfloat16)
    insolation = jnp.clip(20.0 + 80.0 * jax.random.uniform(key_list[2], (NROWS, NCOLS), jnp.float32) ** level_of(key_list[2], (NROWS, NCOLS), ((0, 16), (1, 2)), -0.2, 0.2), 20.0, 100.0).astype(jnp.bfloat16)
    sunlit = draw_sunlit(jax.random.fold_in(key_list[6], 71), 0)
    point_weight = jnp.clip(jnp.exp(jax.random.uniform(key_list[4], (G,), jnp.float32, math.log(0.1), math.log(1.0))), 0.1, 1.0)
    anomaly = gaussian(key_list[5], (NROWS, LEV, NCOLS), 1.0, 6.0, ((0, 16), (2, 2)), jnp.float32)
    return {"optical_depth": optical_depth, "albedo": albedo, "insolation": insolation, "sunlit": sunlit, "point_weight": point_weight, "anomaly": anomaly}


slant_cosine = 0.5
mixing_rate = 0.2
base_loss = 0.005


def radiate(optical_depth, albedo, sunshine, point_weight):
    depth_levels = jnp.moveaxis(optical_depth.astype(jnp.float32), 1, 0)
    albedo_levels = jnp.moveaxis(albedo.astype(jnp.float32), 1, 0)
    albedo_below = jnp.concatenate([albedo_levels[1:], jnp.zeros_like(albedo_levels[:1])], axis=0)
    sun_float = sunshine.astype(jnp.float32)[:, None, :]
    zeros_full = jnp.zeros(depth_levels.shape[1:], jnp.float32)
    zeros_link = jnp.zeros((depth_levels.shape[1], 1, depth_levels.shape[3]), jnp.float32)

    def downward(state_now, layer_in):
        depth_now, link_prev, ratio_prev, swept_prev = state_now
        depth_layer, albedo_now, albedo_next = layer_in
        depth_new = depth_now + depth_layer
        extinct = sun_float * (jnp.exp(-depth_now / slant_cosine) - jnp.exp(-depth_new / slant_cosine))
        link_next = (albedo_now * albedo_next)[:, None, :]
        diagonal = base_loss + 2.0 * (1.0 - albedo_now)[:, None, :] * depth_layer + link_prev + link_next
        pivot = diagonal - link_prev * ratio_prev
        ratio_now = link_next / pivot
        swept_now = (albedo_now[:, None, :] * extinct + link_prev * swept_prev) / pivot
        return (depth_new, link_next, ratio_now, swept_now), (ratio_now, swept_now, extinct)

    init_state = (zeros_full, zeros_link, zeros_full, zeros_full)
    _, (ratios, swept, extinct) = lax.scan(downward, init_state, (depth_levels, albedo_levels, albedo_below))

    def upward(flux_next, layer_in):
        ratio_now, swept_now = layer_in
        diffuse_flux = swept_now + ratio_now * flux_next
        return diffuse_flux, diffuse_flux

    _, diffuse_flux = lax.scan(upward, zeros_full, (ratios, swept), reverse=True)
    absorbed = (1.0 - albedo_levels)[:, :, None, :] * (extinct + 2.0 * depth_levels * diffuse_flux)
    heating = jnp.sum(absorbed * point_weight[None, None, :, None], axis=2)
    return jnp.moveaxis(heating, 0, 1)


def reference(optical_depth, albedo, insolation, sunlit, point_weight, anomaly):
    daylit = jnp.repeat(sunlit, BLOCK, axis=1)
    sunshine = jnp.where(daylit == 1, insolation, jnp.zeros_like(insolation))
    groups = NROWS // ROWS_DEV

    def per_group(inputs):
        return radiate(inputs[0], inputs[1], inputs[2], point_weight)

    heating = lax.map(per_group, (optical_depth.reshape(groups, ROWS_DEV, LEV, G, NCOLS), albedo.reshape(groups, ROWS_DEV, LEV, NCOLS), sunshine.reshape(groups, ROWS_DEV, NCOLS)))
    heating = heating.reshape(NROWS, LEV, NCOLS)
    field_now = anomaly + heating
    for sweep in range(DIFF_STEPS):
        padded = jnp.pad(field_now, ((1, 1), (0, 0), (0, 0)))
        north_south = padded[2:] + padded[:-2]
        east_west = jnp.roll(field_now, 1, axis=2) + jnp.roll(field_now, -1, axis=2)
        field_now = field_now + mixing_rate * (north_south + east_west - 4.0 * field_now)
    return heating, field_now
```

```python
import functools
import math

import jax
import jax.numpy as jnp
import numpy as np
from jax import lax
from jax.experimental import pallas as pl
from jax.experimental.pallas import tpu as pltpu
from jax.sharding import PartitionSpec as P

DIFF_STEPS = 4
HALO = 4
EDGE = 2 * HALO
UNROLL = 3

mixing_rate = 0.2
base_loss = 0.005

MESH = pl.DeviceIdType.MESH
F32 = jnp.float32


def edge_weights(rows):
    full = rows + 2 * HALO
    out = np.zeros((4, 2 * rows * EDGE, rows * EDGE), np.float64)
    columns = [np.ones(1)]
    for _ in range(DIFF_STEPS):
        columns.append(np.convolve(columns[-1], np.ones(3)))
    for variant in range(4):
        near = np.zeros((full, full))
        for i in range(full - 1):
            near[i, i + 1] = near[i + 1, i] = 1.0
        if variant & 1:
            near[:HALO] = 0.0
            near[:, :HALO] = 0.0
        if variant & 2:
            near[-HALO:] = 0.0
            near[:, -HALO:] = 0.0
        for k in range(DIFF_STEPS + 1):
            reach = DIFF_STEPS - k
            power = np.linalg.matrix_power(near, k) * math.comb(DIFF_STEPS, k)
            if k == 0 and variant & 1:
                power[:HALO, :HALO] = 0.0
            if k == 0 and variant & 2:
                power[-HALO:, -HALO:] = 0.0
            for q_to in range(EDGE):
                for q_from in range(EDGE):
                    if (q_to < HALO) == (q_from < HALO):
                        continue
                    gap = abs(q_to - q_from)
                    if gap > reach:
                        continue
                    weight = columns[reach][reach + gap] * mixing_rate**DIFF_STEPS
                    for r_to in range(rows):
                        for r_from in range(full):
                            if r_from < HALO:
                                lane = rows * EDGE + (rows - HALO + r_from) * EDGE
                            elif r_from < HALO + rows:
                                lane = (r_from - HALO) * EDGE
                            else:
                                lane = rows * EDGE + (r_from - HALO - rows) * EDGE
                            out[variant, lane + q_from, r_to * EDGE + q_to] += (
                                weight * power[HALO + r_to, r_from]
                            )
    return out.astype(np.float32)


def kernel(
    n_tiles, n_band, rows, levels, points,
    depth_hbm, albedo_hbm, anomaly_hbm, mats_hbm, insolation, sunlit, weight,
    heat_hbm, smooth_hbm,
    depth_in, albedo_in, anomaly_in, mats, sun, depth_f, albedo_f, swept, ratio, plain, heat_f,
    heat_out, field, smooth, strip, corner, got, got_corner,
    in_sem, out_sem, send_sem, recv_sem,
):
    lanes = field.shape[2]
    tile, band = lax.axis_index("tiles"), lax.axis_index("band")
    has_north, has_south = tile > 0, tile < n_tiles - 1
    north = lax.rem(tile + n_tiles - 1, n_tiles)
    south = lax.rem(tile + 1, n_tiles)
    sides = [lax.rem(band + 1, n_band)]
    if n_band > 2:
        sides.append(lax.rem(band + n_band - 1, n_band))
    n_sides = len(sides)
    per_tile = levels * points
    depth_step = per_tile + 1
    level_step = (levels + 7) // 8 * 8 + 1

    barrier = pltpu.get_barrier_semaphore()

    def greet(to_tile, to_band):
        pl.semaphore_signal(barrier, inc=1, device_id=(to_tile, to_band), device_id_type=MESH)

    for side in sides:
        greet(tile, side)

    @pl.when(has_north)
    def _():
        greet(north, band)
        for side in sides:
            greet(north, side)

    @pl.when(has_south)
    def _():
        greet(south, band)
        for side in sides:
            greet(south, side)

    groups = (((0, HALO), (rows - HALO, HALO)), ((HALO, rows - 2 * HALO),))
    loads = []
    for ranges in groups:
        mine = []
        for first, count in ranges:
            span = pl.ds(first * per_tile, count * per_tile)
            for source, target in (
                (depth_hbm.at[span], depth_in.at[span]),
                (albedo_hbm.at[pl.ds(first, count)], albedo_in.at[pl.ds(first, count)]),
            ):
                mine.append((source, target))
        loads.append(mine)
    copies, number = [], 0
    for mine in loads:
        started = []
        for source, target in mine:
            copy = pltpu.make_async_copy(source, target, in_sem.at[number])
            copy.start()
            started.append(copy)
            number += 1
        copies.append(started)
    anomaly_copy = pltpu.make_async_copy(anomaly_hbm, anomaly_in, in_sem.at[number])
    anomaly_copy.start()
    variant = jnp.where(has_north, 0, 1) + jnp.where(has_south, 0, 2)
    mats_copy = pltpu.make_async_copy(mats_hbm.at[variant], mats, in_sem.at[number + 1])
    mats_copy.start()

    lit = jnp.where(sunlit[...] == 1, insolation[...].astype(F32), 0.0)
    sun[pl.ds(0, HALO), :] = lit[:HALO]
    sun[pl.ds(HALO, HALO), :] = lit[rows - HALO :]
    sun[pl.ds(2 * HALO, rows - 2 * HALO), :] = lit[HALO : rows - HALO]
    weights = [weight[g] for g in range(points)]

    def row_of(slot, group):
        if group == 0:
            return slot if slot < HALO else rows - 2 * HALO + slot
        return HALO + slot

    def radiate(group):
        for copy in copies[group]:
            copy.wait()
        for slot in range(0, 8, 2):
            row = row_of(slot, group)
            pair = depth_in[pl.ds(row * per_tile, 2 * per_tile), :].astype(F32)
            depth_f[pl.ds(slot * depth_step, per_tile), :] = pair[:per_tile]
            depth_f[pl.ds((slot + 1) * depth_step, per_tile), :] = pair[per_tile:]
        for slot in range(8):
            albedo_f[pl.ds(slot * level_step, levels), :] = albedo_in[row_of(slot, group)].astype(F32)
            albedo_f[pl.ds(slot * level_step + levels, 1), :] = jnp.zeros((1, lanes), F32)

        def depth_at(level, g):
            return depth_f[pl.ds(level * points + g, 8, stride=depth_step), :]

        def albedo_at(level):
            return albedo_f[pl.ds(level, 8, stride=level_step), :]

        def down(step, carry):
            for inner in range(UNROLL):
                level = step * UNROLL + inner
                albedo_now, link_prev, state = carry
                albedo_next = albedo_at(level + 1)
                link = albedo_now * albedo_next
                base = base_loss + link_prev + link
                lost = 2.0 - 2.0 * albedo_now
                direct, later = None, []
                for g in range(points):
                    total, beam, p, m, s = state[g]
                    layer = depth_at(level, g)
                    total = total + layer
                    beam_new = jnp.exp(total * -2.0)
                    extinct = beam - beam_new
                    term = weights[g] * extinct
                    direct = term if direct is None else direct + term
                    p_new = (base + lost * layer) * p - link_prev * m
                    m_new = link * p
                    s_new = (albedo_now * extinct) * p + link_prev * s
                    guess = pl.reciprocal(p_new, approx=True)
                    inverse = guess * (2.0 - p_new * guess)
                    swept[level, g] = s_new * inverse
                    ratio[level, g] = m_new * inverse
                    later.append((total, beam_new, p_new, m_new, s_new))
                plain[level] = direct
                carry = (albedo_next, link, tuple(later))
            return carry

        zero = jnp.zeros((8, lanes), F32)
        one = jnp.ones((8, lanes), F32)
        start = (albedo_at(0), zero, tuple((zero, one, one, zero, zero) for _ in range(points)))
        lax.fori_loop(0, levels // UNROLL, down, start)

        sunshine = sun[pl.ds(8 * group, 8), :]

        def up(step, flux):
            for inner in range(UNROLL):
                level = levels - 1 - (step * UNROLL + inner)
                later, absorbed = [], None
                for g in range(points):
                    now = swept[level, g] + ratio[level, g] * flux[g]
                    term = (2.0 * weights[g]) * depth_at(level, g) * now
                    absorbed = term if absorbed is None else absorbed + term
                    later.append(now)
                flux = tuple(later)
                heat = (sunshine - sunshine * albedo_at(level)) * (plain[level] + absorbed)
                heat_f[pl.ds(level, 8, stride=level_step), :] = heat
            return flux

        lax.fori_loop(0, levels // UNROLL, up, tuple(zero for _ in range(points)))
        for slot in range(8):
            row = row_of(slot, group)
            heat = heat_f[pl.ds(slot * level_step, levels), :]
            heat_out[row] = heat
            field[HALO + row] = heat + anomaly_in[row]

    def by_levels(body):
        def step(j, _):
            body(pl.ds(pl.multiple_of(j * 8, 8), 8))
            return 0

        lax.fori_loop(0, levels // 8, step, 0)
        if levels % 8:
            body(pl.ds(levels - 8, 8))

    lane = lax.broadcasted_iota(jnp.int32, (8, lanes), 1)
    lane_row, lane_edge = lane // EDGE, lane % EDGE

    def gather_edges(start, wanted, span):
        value = start
        for place, index in wanted:
            moved = pltpu.roll(field[index, span, :], (place * EDGE + HALO) % lanes, 1)
            value = jnp.where(lane_row == place, moved, value)
        return value

    outer = [(r, HALO + r) for r in (*range(HALO), *range(rows - HALO, rows))]
    inner = [(r, HALO + r) for r in range(HALO, rows - HALO)]

    def remote(source, target, number, to_tile, to_band):
        return pltpu.make_async_remote_copy(
            src_ref=source, dst_ref=target, send_sem=send_sem.at[number], recv_sem=recv_sem.at[number],
            device_id=(to_tile, to_band), device_id_type=MESH,
        )

    to_north = [remote(field.at[pl.ds(HALO, HALO)], field.at[pl.ds(HALO + rows, HALO)], 0, north, band)]
    to_south = [remote(field.at[pl.ds(rows, HALO)], field.at[pl.ds(0, HALO)], 1, south, band)]
    to_side = []
    for j, side in enumerate(sides):
        to_north.append(remote(corner, got_corner.at[0, j], 2 + 3 * j, north, side))
        to_south.append(remote(corner, got_corner.at[1, j], 3 + 3 * j, south, side))
        to_side.append(remote(strip, got.at[j], 4 + 3 * j, tile, side))

    anomaly_copy.wait()
    radiate(0)

    def pack_outer(span):
        corner[span, :] = gather_edges(jnp.zeros((8, lanes), F32), outer, span)

    by_levels(pack_outer)

    peers = n_sides + (1 + n_sides) * (has_north.astype(jnp.int32) + has_south.astype(jnp.int32))
    pl.semaphore_wait(barrier, peers)

    @pl.when(has_north)
    def _():
        for copy in to_north:
            copy.start()

    @pl.when(has_south)
    def _():
        for copy in to_south:
            copy.start()

    @pl.when(jnp.logical_not(has_north))
    def _():
        field[pl.ds(0, HALO)] = jnp.zeros((HALO, levels, lanes), F32)
        for j in range(n_sides):
            got_corner[1, j] = jnp.zeros((levels, lanes), F32)

    @pl.when(jnp.logical_not(has_south))
    def _():
        field[pl.ds(HALO + rows, HALO)] = jnp.zeros((HALO, levels, lanes), F32)
        for j in range(n_sides):
            got_corner[0, j] = jnp.zeros((levels, lanes), F32)

    radiate(1)

    def pack_inner(span):
        strip[span, :] = gather_edges(corner[span, :], inner, span)

    by_levels(pack_inner)
    for copy in to_side:
        copy.start()
    heat_copy = pltpu.make_async_copy(heat_out, heat_hbm, out_sem.at[0])
    heat_copy.start()

    @pl.when(has_north)
    def _():
        for copy in to_south:
            copy.wait_recv()

    @pl.when(has_south)
    def _():
        for copy in to_north:
            copy.wait_recv()

    keep_north = jnp.where(has_north, 1.0, 0.0).astype(F32)
    keep_south = jnp.where(has_south, 1.0, 0.0).astype(F32)
    full = rows + 2 * HALO

    def diffuse(span):
        now = [field[i, span, :] for i in range(full)]
        for sweep in range(1, DIFF_STEPS + 1):
            later = [None] * full
            for i in range(sweep, full - sweep):
                x = now[i]
                value = (x + pltpu.roll(x, 1, 1)) + (pltpu.roll(x, lanes - 1, 1) + (now[i - 1] + now[i + 1]))
                if i < HALO:
                    value = value * keep_north
                if i >= HALO + rows:
                    value = value * keep_south
                later[i] = value
            now = later
        for r in range(rows):
            smooth[r, span, :] = now[HALO + r] * (mixing_rate**DIFF_STEPS)

    by_levels(diffuse)

    mats_copy.wait()
    for copy in to_side:
        copy.wait_recv()

    def pick(ref, span, *lead):
        west = ref[(*lead, 0, span, slice(None))]
        if n_sides == 1:
            return west
        return jnp.where(lane_edge < HALO, west, ref[(*lead, 1, span, slice(None))])

    beyond = [(rows - HALO + i, i) for i in range(HALO)] + [(i, HALO + rows + i) for i in range(HALO)]

    def differ(span):
        here = gather_edges(jnp.zeros((8, lanes), F32), beyond, span)
        there = jnp.where(
            lane_row < HALO,
            pick(got_corner, span, 0),
            jnp.where(lane_row >= rows - HALO, pick(got_corner, span, 1), 0.0),
        )
        return jnp.concatenate([pick(got, span) - strip[span, :], there - here], axis=1)

    def correct(span):
        fix = jnp.dot(
            differ(span), mats[...], precision=lax.Precision.HIGHEST, preferred_element_type=F32
        )
        for r in range(rows):
            moved = pltpu.roll(jnp.where(lane_row == r, fix, 0.0), (2 * lanes - r * EDGE - HALO) % lanes, 1)
            smooth[r, span, :] = smooth[r, span, :] + moved

    def correct_last(span):
        fix = jnp.dot(
            differ(span), mats[...], precision=lax.Precision.HIGHEST, preferred_element_type=F32
        )
        fresh = lax.broadcasted_iota(jnp.int32, (8, lanes), 0) >= 8 - levels % 8
        for r in range(rows):
            chosen = jnp.where((lane_row == r) & fresh, fix, 0.0)
            moved = pltpu.roll(chosen, (2 * lanes - r * EDGE - HALO) % lanes, 1)
            smooth[r, span, :] = smooth[r, span, :] + moved

    def correct_step(j, _):
        correct(pl.ds(pl.multiple_of(j * 8, 8), 8))
        return 0

    lax.fori_loop(0, levels // 8, correct_step, 0)
    if levels % 8:
        correct_last(pl.ds(levels - 8, 8))
    smooth_copy = pltpu.make_async_copy(smooth, smooth_hbm, out_sem.at[1])
    smooth_copy.start()

    @pl.when(has_north)
    def _():
        for copy in to_north:
            copy.wait_send()

    @pl.when(has_south)
    def _():
        for copy in to_south:
            copy.wait_send()

    for copy in to_side:
        copy.wait_send()
    heat_copy.wait()
    smooth_copy.wait()


def per_device(n_tiles, n_band, optical_depth, albedo, insolation, sunlit, point_weight, anomaly):
    rows, levels, points, lanes = optical_depth.shape
    n_sides = 1 if n_band == 2 else 2
    mats = edge_weights(rows)
    level_step = (levels + 7) // 8 * 8 + 1
    shape = jax.ShapeDtypeStruct((rows, levels, lanes), F32)
    vmem, smem, hbm = (pl.BlockSpec(memory_space=m) for m in (pltpu.VMEM, pltpu.SMEM, pl.ANY))
    n_copies = 2 + 3 * n_sides
    return pl.pallas_call(
        functools.partial(kernel, n_tiles, n_band, rows, levels, points),
        out_shape=(shape, shape),
        in_specs=[hbm, hbm, hbm, hbm, vmem, vmem, smem],
        out_specs=(hbm, hbm),
        scratch_shapes=[
            pltpu.VMEM((rows * levels * points, lanes), jnp.bfloat16),
            pltpu.VMEM((rows, levels, lanes), jnp.bfloat16),
            pltpu.VMEM((rows, levels, lanes), F32),
            pltpu.VMEM(mats.shape[1:], F32),
            pltpu.VMEM((rows, lanes), F32),
            pltpu.VMEM((8 * (levels * points + 1), lanes), F32),
            pltpu.VMEM((8 * level_step, lanes), F32),
            pltpu.VMEM((levels, points, 8, lanes), F32),
            pltpu.VMEM((levels, points, 8, lanes), F32),
            pltpu.VMEM((levels, 8, lanes), F32),
            pltpu.VMEM((8 * level_step, lanes), F32),
            pltpu.VMEM((rows, levels, lanes), F32),
            pltpu.VMEM((rows + 2 * HALO, levels, lanes), F32),
            pltpu.VMEM((rows, levels, lanes), F32),
            pltpu.VMEM((levels, lanes), F32),
            pltpu.VMEM((levels, lanes), F32),
            pltpu.VMEM((n_sides, levels, lanes), F32),
            pltpu.VMEM((2, n_sides, levels, lanes), F32),
            pltpu.SemaphoreType.DMA((8,)),
            pltpu.SemaphoreType.DMA((2,)),
            pltpu.SemaphoreType.DMA((n_copies,)),
            pltpu.SemaphoreType.DMA((n_copies,)),
        ],
        compiler_params=pltpu.CompilerParams(
            collective_id=0, has_side_effects=True, vmem_limit_bytes=40 * 1024 * 1024
        ),
    )(
        optical_depth.reshape(rows * levels * points, lanes), albedo, anomaly, jnp.asarray(mats),
        insolation, sunlit, point_weight,
    )


def solution(mesh):
    placed = (
        P("tiles", None, None, "band"),
        P("tiles", None, "band"),
        P("tiles", "band"),
        P("tiles", "band"),
        P(),
        P("tiles", None, "band"),
    )
    return jax.shard_map(
        functools.partial(per_device, mesh.shape["tiles"], mesh.shape["band"]),
        mesh=mesh,
        in_specs=placed,
        out_specs=(P("tiles", None, "band"), P("tiles", None, "band")),
        check_vma=False,
    )
```

```python
import functools
import math

import jax
import jax.numpy as jnp
import numpy as np
from jax import lax
from jax.experimental import pallas as pl
from jax.experimental.pallas import tpu as pltpu
from jax.sharding import PartitionSpec as P

DIFF_STEPS = 4
HALO = 4
EDGE = 2 * HALO
UNROLL = 9

mixing_rate = 0.2
base_loss = 0.005

MESH = pl.DeviceIdType.MESH
F32 = jnp.float32


def edge_weights(rows):
    full = rows + 2 * HALO
    out = np.zeros((4, 2 * rows * EDGE, rows * EDGE), np.float64)
    columns = [np.ones(1)]
    for _ in range(DIFF_STEPS):
        columns.append(np.convolve(columns[-1], np.ones(3)))
    for variant in range(4):
        near = np.zeros((full, full))
        for i in range(full - 1):
            near[i, i + 1] = near[i + 1, i] = 1.0
        if variant & 1:
            near[:HALO] = 0.0
            near[:, :HALO] = 0.0
        if variant & 2:
            near[-HALO:] = 0.0
            near[:, -HALO:] = 0.0
        for k in range(DIFF_STEPS + 1):
            reach = DIFF_STEPS - k
            power = np.linalg.matrix_power(near, k) * math.comb(DIFF_STEPS, k)
            if k == 0 and variant & 1:
                power[:HALO, :HALO] = 0.0
            if k == 0 and variant & 2:
                power[-HALO:, -HALO:] = 0.0
            for q_to in range(EDGE):
                for q_from in range(EDGE):
                    if (q_to < HALO) == (q_from < HALO):
                        continue
                    gap = abs(q_to - q_from)
                    if gap > reach:
                        continue
                    weight = columns[reach][reach + gap] * mixing_rate**DIFF_STEPS
                    for r_to in range(rows):
                        for r_from in range(full):
                            if r_from < HALO:
                                lane = rows * EDGE + (rows - HALO + r_from) * EDGE
                            elif r_from < HALO + rows:
                                lane = (r_from - HALO) * EDGE
                            else:
                                lane = rows * EDGE + (r_from - HALO - rows) * EDGE
                            out[variant, lane + q_from, r_to * EDGE + q_to] += (
                                weight * power[HALO + r_to, r_from]
                            )
    return out.astype(np.float32)


def kernel(
    n_tiles, n_band, rows, levels, points,
    depth_hbm, albedo_hbm, anomaly_hbm, mats_hbm, insolation, sunlit, weight,
    heat_hbm, smooth_hbm,
    depth_in, albedo_in, anomaly_in, mats, depth_f, swept, ratio, plain, heat_held,
    heat_out, field, smooth, smooth_out, strip, corner, got, got_corner,
    in_sem, out_sem, send_sem, recv_sem,
):
    lanes = field.shape[1]
    half = rows // 2
    tile, band = lax.axis_index("tiles"), lax.axis_index("band")
    has_north, has_south = tile > 0, tile < n_tiles - 1
    north = lax.rem(tile + n_tiles - 1, n_tiles)
    south = lax.rem(tile + 1, n_tiles)
    sides = [lax.rem(band + 1, n_band)]
    if n_band > 2:
        sides.append(lax.rem(band + n_band - 1, n_band))
    n_sides = len(sides)
    per_tile = levels * points
    depth_step = per_tile + 1
    slab = (levels + 7) // 8 * 8 + 2
    smooth_step = slab - 1

    barrier = pltpu.get_barrier_semaphore()

    def greet(to_tile, to_band):
        pl.semaphore_signal(barrier, inc=1, device_id=(to_tile, to_band), device_id_type=MESH)

    for side in sides:
        greet(tile, side)

    @pl.when(has_north)
    def _():
        greet(north, band)
        for side in sides:
            greet(north, side)

    @pl.when(has_south)
    def _():
        greet(south, band)
        for side in sides:
            greet(south, side)

    groups = (((0, HALO), (rows - HALO, HALO)), ((HALO, rows - 2 * HALO),))
    loads = []
    for ranges in groups:
        mine = []
        for first, count in ranges:
            span = pl.ds(first * per_tile, count * per_tile)
            mine.append((depth_hbm.at[span], depth_in.at[span]))
        loads.append(mine)
    loads[0].append((albedo_hbm, albedo_in))
    copies, number = [], 0
    for mine in loads:
        started = []
        for source, target in mine:
            copy = pltpu.make_async_copy(source, target, in_sem.at[number])
            copy.start()
            started.append(copy)
            number += 1
        copies.append(started)
    anomaly_copy = pltpu.make_async_copy(anomaly_hbm, anomaly_in, in_sem.at[number])
    anomaly_copy.start()
    variant = jnp.where(has_north, 0, 1) + jnp.where(has_south, 0, 2)
    mats_copy = pltpu.make_async_copy(mats_hbm.at[variant], mats, in_sem.at[number + 1])
    mats_copy.start()

    weights = [weight[g] for g in range(points)]
    sublane = lax.broadcasted_iota(jnp.int32, (half, lanes), 0)
    front = sublane < HALO

    def row_of(slot, group):
        if group == 0:
            return slot if slot < HALO else half + slot
        return half + slot if slot < HALO else slot

    places = {row_of(slot, group): half * group + slot for group in range(2) for slot in range(half)}
    for i in range(HALO):
        places[i - HALO] = rows + i
        places[rows + i] = rows + HALO + i

    def joined(low, high, group):
        return jnp.where(front, low, high) if group == 0 else jnp.where(front, high, low)

    def sunshine_of(group):
        lit = jnp.zeros((half, lanes), jnp.int32)
        for slot in range(half):
            lit = jnp.where(sublane == slot, sunlit[0, row_of(slot, group)], lit)
        sun = insolation[...].astype(F32)
        return jnp.where(lit == 1, joined(sun[:half], sun[half:], group), 0.0)

    def radiate(group):
        for copy in copies[group]:
            copy.wait()
        for slot in range(0, 8, 2):
            row = row_of(slot, group)
            pair = depth_in[pl.ds(row * per_tile, 2 * per_tile), :].astype(F32)
            depth_f[pl.ds(slot * depth_step, per_tile), :] = pair[:per_tile]
            depth_f[pl.ds((slot + 1) * depth_step, per_tile), :] = pair[per_tile:]
        def depth_at(level, g):
            return depth_f[pl.ds(level * points + g, 8, stride=depth_step), :]

        def albedo_at(level):
            pair = albedo_in[pl.ds(pl.multiple_of(level * rows, rows), rows), :].astype(F32)
            return joined(pair[:half], pair[half:], group)

        def down(step, carry):
            for inner in range(UNROLL):
                level = step * UNROLL + inner
                albedo_now, link_prev, state = carry
                albedo_next = albedo_at(jnp.minimum(level + 1, levels - 1))
                albedo_next = jnp.where(level + 1 < levels, albedo_next, 0.0)
                link = albedo_now * albedo_next
                base = base_loss + link_prev + link
                lost = 2.0 - 2.0 * albedo_now
                direct, later = None, []
                for g in range(points):
                    total, beam, p, m, s = state[g]
                    layer = depth_at(level, g)
                    total = total + layer
                    beam_new = jnp.exp(total * -2.0)
                    extinct = beam - beam_new
                    term = weights[g] * extinct
                    direct = term if direct is None else direct + term
                    p_new = (base + lost * layer) * p - link_prev * m
                    m_new = link * p
                    s_new = (albedo_now * extinct) * p + link_prev * s
                    guess = pl.reciprocal(p_new, approx=True)
                    inverse = guess * (2.0 - p_new * guess)
                    swept[level, g] = s_new * inverse
                    ratio[level, g] = m_new * inverse
                    later.append((total, beam_new, p_new, m_new, s_new))
                plain[level] = direct
                carry = (albedo_next, link, tuple(later))
            return carry

        zero = jnp.zeros((8, lanes), F32)
        one = jnp.ones((8, lanes), F32)
        start = (albedo_at(0), zero, tuple((zero, one, one, zero, zero) for _ in range(points)))
        lax.fori_loop(0, levels // UNROLL, down, start)

        sunshine = sunshine_of(group)

        def up(step, flux):
            for inner in range(UNROLL):
                level = levels - 1 - (step * UNROLL + inner)
                later, absorbed = [], None
                for g in range(points):
                    now = swept[level, g] + ratio[level, g] * flux[g]
                    term = (2.0 * weights[g]) * depth_at(level, g) * now
                    absorbed = term if absorbed is None else absorbed + term
                    later.append(now)
                flux = tuple(later)
                heat = (sunshine - sunshine * albedo_at(level)) * (plain[level] + absorbed)
                at = pl.multiple_of(level * rows, rows)
                low, high = pl.ds(at, half), pl.ds(pl.multiple_of(at + half, half), half)
                start = joined(anomaly_in[low, :], anomaly_in[high, :], group)
                field[pl.ds(half * group * slab + level, half, stride=slab), :] = heat + start
                if group == 0:
                    heat_held[level] = heat
                else:
                    other = heat_held[level]
                    heat_out[low, :] = jnp.where(front, other, heat)
                    heat_out[high, :] = jnp.where(front, heat, other)
            return flux

        lax.fori_loop(0, levels // UNROLL, up, tuple(zero for _ in range(points)))

    def by_levels(body):
        def step(j, _):
            body(pl.multiple_of(j * 8, 8))
            return 0

        lax.fori_loop(0, levels // 8, step, 0)
        if levels % 8:
            body(levels - 8)

    def row_levels(row, first):
        return field[pl.ds(places[row] * slab + first, 8), :]

    lane = lax.broadcasted_iota(jnp.int32, (8, lanes), 1)
    lane_row, lane_edge = lane // EDGE, lane % EDGE

    def gather_edges(start, wanted, first):
        value = start
        for place, row in wanted:
            moved = pltpu.roll(row_levels(row, first), (place * EDGE + HALO) % lanes, 1)
            value = jnp.where(lane_row == place, moved, value)
        return value

    outer = [(r, r) for r in (*range(HALO), *range(rows - HALO, rows))]
    inner = [(r, r) for r in range(HALO, rows - HALO)]

    def remote(source, target, number, to_tile, to_band):
        return pltpu.make_async_remote_copy(
            src_ref=source, dst_ref=target, send_sem=send_sem.at[number], recv_sem=recv_sem.at[number],
            device_id=(to_tile, to_band), device_id_type=MESH,
        )

    def slabs(first_row):
        return field.at[pl.ds(places[first_row] * slab, HALO * slab)]

    to_north = [remote(slabs(0), slabs(rows), 0, north, band)]
    to_south = [remote(slabs(rows - HALO), slabs(-HALO), 1, south, band)]
    to_side = []
    for j, side in enumerate(sides):
        to_north.append(remote(corner, got_corner.at[0, j], 2 + 3 * j, north, side))
        to_south.append(remote(corner, got_corner.at[1, j], 3 + 3 * j, south, side))
        to_side.append(remote(strip, got.at[j], 4 + 3 * j, tile, side))

    anomaly_copy.wait()
    radiate(0)

    def pack_outer(first):
        corner[pl.ds(first, 8), :] = gather_edges(jnp.zeros((8, lanes), F32), outer, first)

    by_levels(pack_outer)

    peers = n_sides + (1 + n_sides) * (has_north.astype(jnp.int32) + has_south.astype(jnp.int32))
    pl.semaphore_wait(barrier, peers)

    @pl.when(has_north)
    def _():
        for copy in to_north:
            copy.start()

    @pl.when(has_south)
    def _():
        for copy in to_south:
            copy.start()

    @pl.when(jnp.logical_not(has_north))
    def _():
        slabs(-HALO)[...] = jnp.zeros((HALO * slab, lanes), F32)
        for j in range(n_sides):
            got_corner[1, j] = jnp.zeros((levels, lanes), F32)

    @pl.when(jnp.logical_not(has_south))
    def _():
        slabs(rows)[...] = jnp.zeros((HALO * slab, lanes), F32)
        for j in range(n_sides):
            got_corner[0, j] = jnp.zeros((levels, lanes), F32)

    radiate(1)

    def pack_inner(first):
        span = pl.ds(first, 8)
        strip[span, :] = gather_edges(corner[span, :], inner, first)

    by_levels(pack_inner)
    for copy in to_side:
        copy.start()
    heat_copy = pltpu.make_async_copy(heat_out, heat_hbm, out_sem.at[0])
    heat_copy.start()

    @pl.when(has_north)
    def _():
        for copy in to_south:
            copy.wait_recv()

    @pl.when(has_south)
    def _():
        for copy in to_north:
            copy.wait_recv()

    keep_north = jnp.where(has_north, 1.0, 0.0).astype(F32)
    keep_south = jnp.where(has_south, 1.0, 0.0).astype(F32)
    full = rows + 2 * HALO

    def diffuse(first):
        now = [row_levels(i - HALO, first) for i in range(full)]
        for sweep in range(1, DIFF_STEPS + 1):
            later = [None] * full
            for i in range(sweep, full - sweep):
                x = now[i]
                value = (x + pltpu.roll(x, 1, 1)) + (pltpu.roll(x, lanes - 1, 1) + (now[i - 1] + now[i + 1]))
                if i < HALO:
                    value = value * keep_north
                if i >= HALO + rows:
                    value = value * keep_south
                later[i] = value
            now = later
        for r in range(rows):
            smooth[pl.ds(r * smooth_step + first, 8), :] = now[HALO + r] * (mixing_rate**DIFF_STEPS)

    by_levels(diffuse)

    mats_copy.wait()
    for copy in to_side:
        copy.wait_recv()

    def pick(ref, span, *lead):
        west = ref[(*lead, 0, span, slice(None))]
        if n_sides == 1:
            return west
        return jnp.where(lane_edge < HALO, west, ref[(*lead, 1, span, slice(None))])

    beyond = [(rows - HALO + i, i - HALO) for i in range(HALO)] + [(i, rows + i) for i in range(HALO)]

    def differ(first):
        span = pl.ds(first, 8)
        here = gather_edges(jnp.zeros((8, lanes), F32), beyond, first)
        there = jnp.where(
            lane_row < HALO,
            pick(got_corner, span, 0),
            jnp.where(lane_row >= rows - HALO, pick(got_corner, span, 1), 0.0),
        )
        return jnp.concatenate([pick(got, span) - strip[span, :], there - here], axis=1)

    def correct(first, fresh):
        fix = jnp.dot(
            differ(first), mats[...], precision=lax.Precision.HIGHEST, preferred_element_type=F32
        )
        for r in range(rows):
            chosen = lane_row == r if fresh is None else (lane_row == r) & fresh
            moved = pltpu.roll(jnp.where(chosen, fix, 0.0), (2 * lanes - r * EDGE - HALO) % lanes, 1)
            span = pl.ds(r * smooth_step + first, 8)
            smooth[span, :] = smooth[span, :] + moved

    def correct_step(j, _):
        correct(pl.multiple_of(j * 8, 8), None)
        return 0

    lax.fori_loop(0, levels // 8, correct_step, 0)
    if levels % 8:
        correct(levels - 8, sublane >= 8 - levels % 8)

    def put_back(step, _):
        for inner in range(UNROLL):
            level = step * UNROLL + inner
            for part in range(2):
                value = smooth[pl.ds(part * half * smooth_step + level, half, stride=smooth_step), :]
                smooth_out[pl.ds(pl.multiple_of(level * rows + part * half, half), half), :] = value
        return 0

    lax.fori_loop(0, levels // UNROLL, put_back, 0)
    smooth_copy = pltpu.make_async_copy(smooth_out, smooth_hbm, out_sem.at[1])
    smooth_copy.start()

    @pl.when(has_north)
    def _():
        for copy in to_north:
            copy.wait_send()

    @pl.when(has_south)
    def _():
        for copy in to_south:
            copy.wait_send()

    for copy in to_side:
        copy.wait_send()
    heat_copy.wait()
    smooth_copy.wait()


def per_device(n_tiles, n_band, optical_depth, albedo, insolation, sunlit, point_weight, anomaly):
    rows, levels, points, lanes = optical_depth.shape
    n_sides = 1 if n_band == 2 else 2
    mats = edge_weights(rows)
    slab = (levels + 7) // 8 * 8 + 2

    def by_level(x):
        return jnp.swapaxes(x, 0, 1).reshape(levels * rows, lanes)

    shape = jax.ShapeDtypeStruct((levels * rows, lanes), F32)
    vmem, smem, hbm = (pl.BlockSpec(memory_space=m) for m in (pltpu.VMEM, pltpu.SMEM, pl.ANY))
    n_copies = 2 + 3 * n_sides
    heating, smoothed = pl.pallas_call(
        functools.partial(kernel, n_tiles, n_band, rows, levels, points),
        out_shape=(shape, shape),
        in_specs=[hbm, hbm, hbm, hbm, vmem, smem, smem],
        out_specs=(hbm, hbm),
        scratch_shapes=[
            pltpu.VMEM((rows * levels * points, lanes), jnp.bfloat16),
            pltpu.VMEM((levels * rows, lanes), jnp.bfloat16),
            pltpu.VMEM((levels * rows, lanes), F32),
            pltpu.VMEM(mats.shape[1:], F32),
            pltpu.VMEM((8 * (levels * points + 1), lanes), F32),
            pltpu.VMEM((levels, points, 8, lanes), F32),
            pltpu.VMEM((levels, points, 8, lanes), F32),
            pltpu.VMEM((levels, 8, lanes), F32),
            pltpu.VMEM((levels, 8, lanes), F32),
            pltpu.VMEM((levels * rows, lanes), F32),
            pltpu.VMEM(((rows + 2 * HALO) * slab, lanes), F32),
            pltpu.VMEM((rows * (slab - 1), lanes), F32),
            pltpu.VMEM((levels * rows, lanes), F32),
            pltpu.VMEM((levels, lanes), F32),
            pltpu.VMEM((levels, lanes), F32),
            pltpu.VMEM((n_sides, levels, lanes), F32),
            pltpu.VMEM((2, n_sides, levels, lanes), F32),
            pltpu.SemaphoreType.DMA((8,)),
            pltpu.SemaphoreType.DMA((2,)),
            pltpu.SemaphoreType.DMA((n_copies,)),
            pltpu.SemaphoreType.DMA((n_copies,)),
        ],
        compiler_params=pltpu.CompilerParams(
            collective_id=0, has_side_effects=True, vmem_limit_bytes=56 * 1024 * 1024
        ),
    )(
        optical_depth.reshape(rows * levels * points, lanes),
        by_level(albedo), by_level(anomaly), jnp.asarray(mats), insolation, sunlit.T, point_weight,
    )
    return tuple(jnp.swapaxes(x.reshape(levels, rows, lanes), 0, 1) for x in (heating, smoothed))


def solution(mesh):
    placed = (
        P("tiles", None, None, "band"),
        P("tiles", None, "band"),
        P("tiles", "band"),
        P("tiles", "band"),
        P(),
        P("tiles", None, "band"),
    )
    return jax.shard_map(
        functools.partial(per_device, mesh.shape["tiles"], mesh.shape["band"]),
        mesh=mesh,
        in_specs=placed,
        out_specs=(P("tiles", None, "band"), P("tiles", None, "band")),
        check_vma=False,
    )
```

```python
import functools
import math

import jax
import jax.numpy as jnp
import numpy as np
from jax import lax
from jax.experimental import pallas as pl
from jax.experimental.pallas import tpu as pltpu
from jax.sharding import PartitionSpec as P

DIFF_STEPS = 4
HALO = 4
EDGE = 2 * HALO
UNROLL = 9
CHUNK = 24

mixing_rate = 0.2
base_loss = 0.005

MESH = pl.DeviceIdType.MESH
F32 = jnp.float32


def edge_weights(rows):
    full = rows + 2 * HALO
    out = np.zeros((4, 2 * rows * EDGE, rows * EDGE), np.float64)
    columns = [np.ones(1)]
    for _ in range(DIFF_STEPS):
        columns.append(np.convolve(columns[-1], np.ones(3)))
    for variant in range(4):
        near = np.zeros((full, full))
        for i in range(full - 1):
            near[i, i + 1] = near[i + 1, i] = 1.0
        if variant & 1:
            near[:HALO] = 0.0
            near[:, :HALO] = 0.0
        if variant & 2:
            near[-HALO:] = 0.0
            near[:, -HALO:] = 0.0
        for k in range(DIFF_STEPS + 1):
            reach = DIFF_STEPS - k
            power = np.linalg.matrix_power(near, k) * math.comb(DIFF_STEPS, k)
            if k == 0 and variant & 1:
                power[:HALO, :HALO] = 0.0
            if k == 0 and variant & 2:
                power[-HALO:, -HALO:] = 0.0
            for q_to in range(EDGE):
                for q_from in range(EDGE):
                    if (q_to < HALO) == (q_from < HALO):
                        continue
                    gap = abs(q_to - q_from)
                    if gap > reach:
                        continue
                    weight = columns[reach][reach + gap]
                    for r_to in range(rows):
                        for r_from in range(full):
                            if r_from < HALO:
                                lane = (rows + r_from) * EDGE
                            elif r_from < HALO + rows:
                                lane = (r_from - HALO) * EDGE
                            else:
                                lane = r_from * EDGE
                            out[variant, lane + q_from, r_to * EDGE + q_to] += (
                                weight * power[HALO + r_to, r_from]
                            )
    return out.astype(jnp.bfloat16)


def kernel(
    n_tiles, n_band, rows, levels, points,
    depth_hbm, albedo_hbm, anomaly_hbm, mats_hbm, insolation, sunlit, weight,
    heat_out, smooth, fix,
    depth_in, albedo_in, anomaly_in, mats, depth_f, swept, ratio, plain, heat_held,
    field, strip, corner, got, got_corner, differ,
    in_sem, send_sem, recv_sem,
):
    lanes = field.shape[1]
    half = rows // 2
    tile, band = lax.axis_index("tiles"), lax.axis_index("band")
    has_north, has_south = tile > 0, tile < n_tiles - 1
    north = lax.rem(tile + n_tiles - 1, n_tiles)
    south = lax.rem(tile + 1, n_tiles)
    sides = [lax.rem(band + 1, n_band)]
    if n_band > 2:
        sides.append(lax.rem(band + n_band - 1, n_band))
    n_sides = len(sides)
    per_tile = levels * points
    depth_step = per_tile + 1
    slab = (levels + 7) // 8 * 8 + 2
    smooth_step = slab - 1

    barrier = pltpu.get_barrier_semaphore()

    def greet(to_tile, to_band):
        pl.semaphore_signal(barrier, inc=1, device_id=(to_tile, to_band), device_id_type=MESH)

    for side in sides:
        greet(tile, side)

    @pl.when(has_north)
    def _():
        greet(north, band)
        for side in sides:
            greet(north, side)

    @pl.when(has_south)
    def _():
        greet(south, band)
        for side in sides:
            greet(south, side)

    groups = (((0, HALO), (rows - HALO, HALO)), ((HALO, rows - 2 * HALO),))
    loads = []
    for ranges in groups:
        mine = []
        for first, count in ranges:
            span = pl.ds(first * per_tile, count * per_tile)
            mine.append((depth_hbm.at[span], depth_in.at[span]))
        loads.append(mine)
    loads[0].append((albedo_hbm, albedo_in))
    copies, number = [], 0
    for mine in loads:
        started = []
        for source, target in mine:
            copy = pltpu.make_async_copy(source, target, in_sem.at[number])
            copy.start()
            started.append(copy)
            number += 1
        copies.append(started)
    anomaly_copy = pltpu.make_async_copy(anomaly_hbm, anomaly_in, in_sem.at[number])
    anomaly_copy.start()
    variant = jnp.where(has_north, 0, 1) + jnp.where(has_south, 0, 2)
    mats_copy = pltpu.make_async_copy(mats_hbm.at[variant], mats, in_sem.at[number + 1])
    mats_copy.start()

    weights = [weight[g] for g in range(points)]
    sublane = lax.broadcasted_iota(jnp.int32, (half, lanes), 0)
    front = sublane < HALO

    def row_of(slot, group):
        if group == 0:
            return slot if slot < HALO else half + slot
        return half + slot if slot < HALO else slot

    places = {row_of(slot, group): half * group + slot for group in range(2) for slot in range(half)}
    for i in range(HALO):
        places[i - HALO] = rows + i
        places[rows + i] = rows + HALO + i

    def joined(low, high, group):
        return jnp.where(front, low, high) if group == 0 else jnp.where(front, high, low)

    def sunshine_of(group):
        lit = jnp.zeros((half, lanes), jnp.int32)
        for slot in range(half):
            lit = jnp.where(sublane == slot, sunlit[0, row_of(slot, group)], lit)
        sun = insolation[...].astype(F32)
        return jnp.where(lit == 1, joined(sun[:half], sun[half:], group), 0.0)

    def radiate(group):
        for copy in copies[group]:
            copy.wait()
        for slot in range(0, 8, 2):
            row = row_of(slot, group)
            pair = depth_in[pl.ds(row * per_tile, 2 * per_tile), :].astype(F32)
            depth_f[pl.ds(slot * depth_step, per_tile), :] = pair[:per_tile]
            depth_f[pl.ds((slot + 1) * depth_step, per_tile), :] = pair[per_tile:]
        def depth_at(level, g):
            return depth_f[pl.ds(level * points + g, 8, stride=depth_step), :]

        def albedo_at(level):
            pair = albedo_in[pl.ds(pl.multiple_of(level * rows, rows), rows), :].astype(F32)
            return joined(pair[:half], pair[half:], group)

        def down(step, carry):
            for inner in range(UNROLL):
                level = step * UNROLL + inner
                albedo_now, link_prev, state = carry
                albedo_next = albedo_at(jnp.minimum(level + 1, levels - 1))
                albedo_next = jnp.where(level + 1 < levels, albedo_next, 0.0)
                link = albedo_now * albedo_next
                base = base_loss + link_prev + link
                lost = 2.0 - 2.0 * albedo_now
                direct, later = None, []
                for g in range(points):
                    total, beam, p, m, s = state[g]
                    layer = depth_at(level, g)
                    total = total + layer
                    beam_new = jnp.exp(total * -2.0)
                    extinct = beam - beam_new
                    term = weights[g] * extinct
                    direct = term if direct is None else direct + term
                    p_new = (base + lost * layer) * p - link_prev * m
                    m_new = link * p
                    s_new = (albedo_now * extinct) * p + link_prev * s
                    guess = pl.reciprocal(p_new, approx=True)
                    inverse = guess * (2.0 - p_new * guess)
                    swept[level, g] = s_new * inverse
                    ratio[level, g] = m_new * inverse
                    later.append((total, beam_new, p_new, m_new, s_new))
                plain[level] = direct
                carry = (albedo_next, link, tuple(later))
            return carry

        zero = jnp.zeros((8, lanes), F32)
        one = jnp.ones((8, lanes), F32)
        start = (albedo_at(0), zero, tuple((zero, one, one, zero, zero) for _ in range(points)))
        lax.fori_loop(0, levels // UNROLL, down, start)

        sunshine = sunshine_of(group)

        def up(step, flux):
            for inner in range(UNROLL):
                level = levels - 1 - (step * UNROLL + inner)
                later, absorbed = [], None
                for g in range(points):
                    now = swept[level, g] + ratio[level, g] * flux[g]
                    term = (2.0 * weights[g]) * depth_at(level, g) * now
                    absorbed = term if absorbed is None else absorbed + term
                    later.append(now)
                flux = tuple(later)
                heat = (sunshine - sunshine * albedo_at(level)) * (plain[level] + absorbed)
                at = pl.multiple_of(level * rows, rows)
                low, high = pl.ds(at, half), pl.ds(pl.multiple_of(at + half, half), half)
                start = joined(anomaly_in[low, :], anomaly_in[high, :], group)
                field[pl.ds(half * group * slab + level, half, stride=slab), :] = heat + start
                if group == 0:
                    heat_held[level] = heat
                else:
                    other = heat_held[level]
                    heat_out[low, :] = jnp.where(front, other, heat)
                    heat_out[high, :] = jnp.where(front, heat, other)
            return flux

        lax.fori_loop(0, levels // UNROLL, up, tuple(zero for _ in range(points)))

    def by_levels(body):
        def step(j, _):
            body(pl.multiple_of(j * 8, 8))
            return 0

        lax.fori_loop(0, levels // 8, step, 0)
        if levels % 8:
            body(levels - 8)

    def row_levels(row, first):
        return field[pl.ds(places[row] * slab + first, 8), :]

    lane = lax.broadcasted_iota(jnp.int32, (8, lanes), 1)
    lane_row, lane_edge = lane // EDGE, lane % EDGE

    def gather_edges(start, wanted, first):
        value = start
        for place, row in wanted:
            moved = pltpu.roll(row_levels(row, first), (place * EDGE + HALO) % lanes, 1)
            value = jnp.where(lane_row == place, moved, value)
        return value

    blocks = [*range(0, levels - 7, 8)] + ([levels - 8] if levels % 8 else [])
    outer = [(r, r) for r in (*range(HALO), *range(rows - HALO, rows))]
    inner = [(r, r) for r in range(HALO, rows - HALO)]

    def remote(source, target, number, to_tile, to_band):
        return pltpu.make_async_remote_copy(
            src_ref=source, dst_ref=target, send_sem=send_sem.at[number], recv_sem=recv_sem.at[number],
            device_id=(to_tile, to_band), device_id_type=MESH,
        )

    def slabs(first_row):
        return field.at[pl.ds(places[first_row] * slab, HALO * slab)]

    to_north = [remote(slabs(0), slabs(rows), 0, north, band)]
    to_south = [remote(slabs(rows - HALO), slabs(-HALO), 1, south, band)]
    to_side = []
    for j, side in enumerate(sides):
        to_north.append(remote(corner.at[0], got_corner.at[0, j], 2 + 3 * j, north, side))
        to_south.append(remote(corner.at[1], got_corner.at[1, j], 3 + 3 * j, south, side))
        to_side.append(remote(strip, got.at[j], 4 + 3 * j, tile, side))

    anomaly_copy.wait()
    radiate(0)

    def pack_corner(first_row):
        packed = []
        for j, first in enumerate(blocks):
            if j % HALO == 0:
                packed.append(jnp.zeros((8, lanes), F32))
            wanted = [(j % HALO * HALO + i, first_row + i) for i in range(HALO)]
            packed[-1] = gather_edges(packed[-1], wanted, first)
        return packed

    for end, first_row in enumerate((0, rows - HALO)):
        for v, value in enumerate(pack_corner(first_row)):
            corner[end, v] = value

    peers = n_sides + (1 + n_sides) * (has_north.astype(jnp.int32) + has_south.astype(jnp.int32))
    pl.semaphore_wait(barrier, peers)

    @pl.when(has_north)
    def _():
        for copy in to_north:
            copy.start()

    @pl.when(has_south)
    def _():
        for copy in to_south:
            copy.start()

    @pl.when(jnp.logical_not(has_north))
    def _():
        slabs(-HALO)[...] = jnp.zeros((HALO * slab, lanes), F32)
        for j in range(n_sides):
            got_corner[1, j] = jnp.zeros(corner.shape[1:], F32)

    @pl.when(jnp.logical_not(has_south))
    def _():
        slabs(rows)[...] = jnp.zeros((HALO * slab, lanes), F32)
        for j in range(n_sides):
            got_corner[0, j] = jnp.zeros(corner.shape[1:], F32)

    def pack_outer(first):
        strip[pl.ds(first, 8), :] = gather_edges(jnp.zeros((8, lanes), F32), outer, first)

    def pack_inner(first):
        span = pl.ds(first, 8)
        strip[span, :] = gather_edges(strip[span, :], inner, first)

    by_levels(pack_outer)
    radiate(1)
    by_levels(pack_inner)
    for copy in to_side:
        copy.start()

    @pl.when(has_north)
    def _():
        for copy in to_south:
            copy.wait_recv()

    @pl.when(has_south)
    def _():
        for copy in to_north:
            copy.wait_recv()

    keep_north = jnp.where(has_north, 1.0, 0.0).astype(F32)
    keep_south = jnp.where(has_south, 1.0, 0.0).astype(F32)
    full = rows + 2 * HALO

    def diffuse(first):
        now = [row_levels(i - HALO, first) for i in range(full)]
        for sweep in range(1, DIFF_STEPS + 1):
            later = [None] * full
            for i in range(sweep, full - sweep):
                x = now[i]
                value = (x + pltpu.roll(x, 1, 1)) + (pltpu.roll(x, lanes - 1, 1) + (now[i - 1] + now[i + 1]))
                if i < HALO:
                    value = value * keep_north
                if i >= HALO + rows:
                    value = value * keep_south
                later[i] = value
            now = later
        for r in range(rows):
            smooth[pl.ds(r * smooth_step + first, 8), :] = now[HALO + r] * (mixing_rate**DIFF_STEPS)

    by_levels(diffuse)

    mats_copy.wait()
    for copy in to_side:
        copy.wait_recv()

    def pick(ref, *at):
        west = ref[(*at[:-1], 0, at[-1])]
        if n_sides == 1:
            return west
        return jnp.where(lane_edge < HALO, west, ref[(*at[:-1], 1, at[-1])])

    ends = []
    for end, first_row in ((1, -HALO), (0, rows)):
        ends.append([pick(got_corner, end, v) - here for v, here in enumerate(pack_corner(first_row))])
    differ[pl.ds(differ.shape[0] - 8, 8), :] = jnp.zeros((8, 2 * lanes), F32)
    width = HALO * EDGE
    for j, first in enumerate(blocks):
        span = pl.ds(first, 8)
        differ[span, pl.ds(0, lanes)] = pick(got, span) - strip[span, :]
        above, below = (x[j // HALO] for x in ends)
        above = pltpu.roll(above, (lanes - j % HALO * width) % lanes, 1)
        below = pltpu.roll(below, (lanes + width - j % HALO * width) % lanes, 1)
        beyond = jnp.where(lane < width, above, jnp.where(lane < 2 * width, below, 0.0))
        differ[span, pl.ds(lanes, lanes)] = beyond
    rest, total = differ[...], None
    for _ in range(3):
        part = rest.astype(jnp.bfloat16)
        rest = rest - part.astype(F32)
        term = jnp.dot(part, mats[...], preferred_element_type=F32)
        total = term if total is None else total + term
    fix[...] = total * (mixing_rate**DIFF_STEPS)

    @pl.when(has_north)
    def _():
        for copy in to_north:
            copy.wait_send()

    @pl.when(has_south)
    def _():
        for copy in to_south:
            copy.wait_send()

    for copy in to_side:
        copy.wait_send()


def finish(rows, levels, heat, smooth, fix, heat_hbm, smooth_hbm, fixed, ordered, sem):
    lanes = heat.shape[1]
    half = rows // 2
    step = smooth.shape[0] // rows
    heat_copy = pltpu.make_async_copy(heat, heat_hbm, sem.at[0])
    heat_copy.start()
    lane_row = lax.broadcasted_iota(jnp.int32, (8, lanes), 1) // EDGE
    copies, done = [heat_copy], 0
    for first in [*range(0, levels - 7, 8)] + ([levels - 8] if levels % 8 else []):
        value = fix[pl.ds(first, 8), :]
        for r in range(rows):
            moved = pltpu.roll(jnp.where(lane_row == r, value, 0.0), (2 * lanes - r * EDGE - HALO) % lanes, 1)
            span = pl.ds(r * step + first, 8)
            fixed[span, :] = smooth[span, :] + moved
        if first + 8 - done < CHUNK and first + 8 < levels:
            continue
        for level in range(done, first + 8):
            for part in range(2):
                eight = fixed[pl.ds(part * half * step + level, half, stride=step), :]
                ordered[pl.ds(level * rows + part * half, half), :] = eight
        span = pl.ds(done * rows, (first + 8 - done) * rows)
        copy = pltpu.make_async_copy(ordered.at[span], smooth_hbm.at[span], sem.at[len(copies)])
        copy.start()
        copies.append(copy)
        done = first + 8
    for copy in copies:
        copy.wait()


def per_device(n_tiles, n_band, optical_depth, albedo, insolation, sunlit, point_weight, anomaly):
    rows, levels, points, lanes = optical_depth.shape
    n_sides = 1 if n_band == 2 else 2
    mats = edge_weights(rows)
    slab = (levels + 7) // 8 * 8 + 2

    def by_level(x):
        return jnp.swapaxes(x, 0, 1).reshape(levels * rows, lanes)

    shape = jax.ShapeDtypeStruct((levels * rows, lanes), F32)
    vmem, smem, hbm = (pl.BlockSpec(memory_space=m) for m in (pltpu.VMEM, pltpu.SMEM, pltpu.HBM))
    n_copies = 2 + 3 * n_sides
    deep = (levels + 7) // 8 * 8
    heat, smooth, fix = pl.pallas_call(
        functools.partial(kernel, n_tiles, n_band, rows, levels, points),
        out_shape=(
            shape,
            jax.ShapeDtypeStruct((rows * (slab - 1), lanes), F32),
            jax.ShapeDtypeStruct((deep, lanes), F32),
        ),
        in_specs=[hbm, hbm, hbm, hbm, vmem, smem, smem],
        out_specs=(vmem, vmem, vmem),
        scratch_shapes=[
            pltpu.VMEM((rows * levels * points, lanes), jnp.bfloat16),
            pltpu.VMEM((levels * rows, lanes), jnp.bfloat16),
            pltpu.VMEM((levels * rows, lanes), F32),
            pltpu.VMEM(mats.shape[1:], jnp.bfloat16),
            pltpu.VMEM((8 * (levels * points + 1), lanes), F32),
            pltpu.VMEM((levels, points, 8, lanes), F32),
            pltpu.VMEM((levels, points, 8, lanes), F32),
            pltpu.VMEM((levels, 8, lanes), F32),
            pltpu.VMEM((levels, 8, lanes), F32),
            pltpu.VMEM(((rows + 2 * HALO) * slab, lanes), F32),
            pltpu.VMEM((levels, lanes), F32),
            pltpu.VMEM((2, deep // 32, 8, lanes), F32),
            pltpu.VMEM((n_sides, levels, lanes), F32),
            pltpu.VMEM((2, n_sides, deep // 32, 8, lanes), F32),
            pltpu.VMEM((deep, 2 * lanes), F32),
            pltpu.SemaphoreType.DMA((8,)),
            pltpu.SemaphoreType.DMA((n_copies,)),
            pltpu.SemaphoreType.DMA((n_copies,)),
        ],
        compiler_params=pltpu.CompilerParams(
            collective_id=0, has_side_effects=True, vmem_limit_bytes=20 * 1024 * 1024
        ),
    )(
        optical_depth.reshape(rows * levels * points, lanes),
        by_level(albedo), by_level(anomaly), jnp.asarray(mats), insolation, sunlit.T, point_weight,
    )
    heating, smoothed = pl.pallas_call(
        functools.partial(finish, rows, levels),
        out_shape=(shape, shape),
        in_specs=[vmem, vmem, vmem],
        out_specs=(hbm, hbm),
        scratch_shapes=[
            pltpu.VMEM((rows * (slab - 1), lanes), F32),
            pltpu.VMEM((levels * rows, lanes), F32),
            pltpu.SemaphoreType.DMA((2 + levels // CHUNK + 1,)),
        ],
        compiler_params=pltpu.CompilerParams(vmem_limit_bytes=20 * 1024 * 1024),
    )(heat, smooth, fix)
    return tuple(jnp.swapaxes(x.reshape(levels, rows, lanes), 0, 1) for x in (heating, smoothed))


def solution(mesh):
    placed = (
        P("tiles", None, None, "band"),
        P("tiles", None, "band"),
        P("tiles", "band"),
        P("tiles", "band"),
        P(),
        P("tiles", None, "band"),
    )
    return jax.shard_map(
        functools.partial(per_device, mesh.shape["tiles"], mesh.shape["band"]),
        mesh=mesh,
        in_specs=placed,
        out_specs=(P("tiles", None, "band"), P("tiles", None, "band")),
        check_vma=False,
    )
```

```python
import functools
import math

import jax
import jax.numpy as jnp
import numpy as np
from jax import lax
from jax.experimental import pallas as pl
from jax.experimental.pallas import tpu as pltpu
from jax.sharding import PartitionSpec as P

DIFF_STEPS = 4
HALO = 4
EDGE = 2 * HALO
UNROLL = 18
TOGETHER = 3
CHUNK = 24

mixing_rate = 0.2
base_loss = 0.005

MESH = pl.DeviceIdType.MESH
F32 = jnp.float32


def edge_weights(rows):
    full = rows + 2 * HALO
    out = np.zeros((4, 2 * rows * EDGE, rows * EDGE), np.float64)
    columns = [np.ones(1)]
    for _ in range(DIFF_STEPS):
        columns.append(np.convolve(columns[-1], np.ones(3)))
    for variant in range(4):
        near = np.zeros((full, full))
        for i in range(full - 1):
            near[i, i + 1] = near[i + 1, i] = 1.0
        if variant & 1:
            near[:HALO] = 0.0
            near[:, :HALO] = 0.0
        if variant & 2:
            near[-HALO:] = 0.0
            near[:, -HALO:] = 0.0
        for k in range(DIFF_STEPS + 1):
            reach = DIFF_STEPS - k
            power = np.linalg.matrix_power(near, k) * math.comb(DIFF_STEPS, k)
            if k == 0 and variant & 1:
                power[:HALO, :HALO] = 0.0
            if k == 0 and variant & 2:
                power[-HALO:, -HALO:] = 0.0
            for q_to in range(EDGE):
                for q_from in range(EDGE):
                    if (q_to < HALO) == (q_from < HALO):
                        continue
                    gap = abs(q_to - q_from)
                    if gap > reach:
                        continue
                    weight = columns[reach][reach + gap]
                    for r_to in range(rows):
                        for r_from in range(full):
                            if r_from < HALO:
                                lane = (rows + r_from) * EDGE
                            elif r_from < HALO + rows:
                                lane = (r_from - HALO) * EDGE
                            else:
                                lane = r_from * EDGE
                            out[variant, lane + q_from, r_to * EDGE + q_to] += (
                                weight * power[HALO + r_to, r_from]
                            )
    return out.astype(jnp.bfloat16)


def kernel(
    n_tiles, n_band, rows, levels, points,
    depth_hbm, albedo_hbm, anomaly_hbm, mats_hbm, insolation_hbm, sunlit_hbm, weight_hbm,
    heat_hbm, smooth_hbm, fix_hbm,
    depth_in, albedo_in, anomaly_in, mats, insolation, sunlit, weight, depth_f, swept, ratio, plain, heat_held,
    heat_out, smooth, fix, field, strip, corner, got, got_corner, differ,
    in_sem, out_sem, send_sem, recv_sem,
):
    lanes = field.shape[1]
    half = rows // 2
    tile, band = lax.axis_index("tiles"), lax.axis_index("band")
    has_north, has_south = tile > 0, tile < n_tiles - 1
    north = lax.rem(tile + n_tiles - 1, n_tiles)
    south = lax.rem(tile + 1, n_tiles)
    sides = [lax.rem(band + 1, n_band)]
    if n_band > 2:
        sides.append(lax.rem(band + n_band - 1, n_band))
    n_sides = len(sides)
    per_tile = levels * points
    depth_step = per_tile + 1
    slab = (levels + 7) // 8 * 8 + 2
    smooth_step = slab - 1

    barrier = pltpu.get_barrier_semaphore()

    def greet(to_tile, to_band):
        pl.semaphore_signal(barrier, inc=1, device_id=(to_tile, to_band), device_id_type=MESH)

    for side in sides:
        greet(tile, side)

    @pl.when(has_north)
    def _():
        greet(north, band)
        for side in sides:
            greet(north, side)

    @pl.when(has_south)
    def _():
        greet(south, band)
        for side in sides:
            greet(south, side)

    groups = (((0, HALO), (rows - HALO, HALO)), ((HALO, rows - 2 * HALO),))
    loads = []
    for ranges in groups:
        mine = []
        for first, count in ranges:
            span = pl.ds(first * per_tile, count * per_tile)
            mine.append((depth_hbm.at[span], depth_in.at[span]))
        loads.append(mine)
    loads[0] += [(albedo_hbm, albedo_in), (insolation_hbm, insolation), (sunlit_hbm, sunlit), (weight_hbm, weight)]
    copies, number = [], 0
    for mine in loads:
        started = []
        for source, target in mine:
            copy = pltpu.make_async_copy(source, target, in_sem.at[number])
            copy.start()
            started.append(copy)
            number += 1
        copies.append(started)
    anomaly_copy = pltpu.make_async_copy(anomaly_hbm, anomaly_in, in_sem.at[number])
    anomaly_copy.start()
    variant = jnp.where(has_north, 0, 1) + jnp.where(has_south, 0, 2)
    mats_copy = pltpu.make_async_copy(mats_hbm.at[variant], mats, in_sem.at[number + 1])
    mats_copy.start()

    sublane = lax.broadcasted_iota(jnp.int32, (half, lanes), 0)
    front = sublane < HALO

    def row_of(slot, group):
        if group == 0:
            return slot if slot < HALO else half + slot
        return half + slot if slot < HALO else slot

    places = {row_of(slot, group): half * group + slot for group in range(2) for slot in range(half)}
    for i in range(HALO):
        places[i - HALO] = rows + i
        places[rows + i] = rows + HALO + i

    def joined(low, high, group):
        return jnp.where(front, low, high) if group == 0 else jnp.where(front, high, low)

    def sunshine_of(group):
        lit = jnp.zeros((half, lanes), jnp.int32)
        for slot in range(half):
            lit = jnp.where(sublane == slot, sunlit[0, row_of(slot, group)], lit)
        sun = insolation[...].astype(F32)
        return jnp.where(lit == 1, joined(sun[:half], sun[half:], group), 0.0)

    def radiate(group):
        for copy in copies[group]:
            copy.wait()
        weights = [weight[g] for g in range(points)]
        for slot in range(0, 8, 2):
            row = row_of(slot, group)
            pair = depth_in[pl.ds(row * per_tile, 2 * per_tile), :].astype(F32)
            depth_f[pl.ds(slot * depth_step, per_tile), :] = pair[:per_tile]
            depth_f[pl.ds((slot + 1) * depth_step, per_tile), :] = pair[per_tile:]
        def depth_at(level, g):
            return depth_f[pl.ds(level * points + g, 8, stride=depth_step), :]

        def albedo_at(level):
            pair = albedo_in[pl.ds(pl.multiple_of(level * rows, rows), rows), :].astype(F32)
            return joined(pair[:half], pair[half:], group)

        def down(step, carry):
            for inner in range(UNROLL):
                level = step * UNROLL + inner
                albedo_now, link_prev, state = carry
                albedo_next = albedo_at(jnp.minimum(level + 1, levels - 1))
                albedo_next = jnp.where(level + 1 < levels, albedo_next, 0.0)
                link = albedo_now * albedo_next
                base = base_loss + link_prev + link
                lost = 2.0 - 2.0 * albedo_now
                direct, later = None, []
                for g in range(points):
                    total, beam, p, m, s = state[g]
                    layer = depth_at(level, g)
                    total = total + layer * exponent
                    beam_new = weights[g] * jnp.exp2(total)
                    extinct = beam - beam_new
                    direct = extinct if direct is None else direct + extinct
                    p_new = (base + lost * layer) * p - link_prev * m
                    m_new = link * p
                    s_new = (albedo_now * extinct) * p + link_prev * s
                    guess = pl.reciprocal(p_new, approx=True)
                    inverse = guess * (2.0 - p_new * guess)
                    swept[level, g] = s_new * inverse
                    ratio[level, g] = m_new * inverse
                    later.append((total, beam_new, p_new, m_new, s_new))
                plain[level] = direct
                carry = (albedo_next, link, tuple(later))
            return carry

        exponent = -2.0 / math.log(2.0)
        zero = jnp.zeros((8, lanes), F32)
        one = jnp.ones((8, lanes), F32)
        start = (albedo_at(0), zero, tuple((zero, weights[g] * one, one, zero, zero) for g in range(points)))
        lax.fori_loop(0, levels // UNROLL, down, start)

        sunshine = sunshine_of(group)

        def up(step, flux):
            for inner in range(UNROLL):
                level = levels - 1 - (step * UNROLL + inner)
                later, absorbed = [], None
                for g in range(points):
                    now = swept[level, g] + ratio[level, g] * flux[g]
                    term = depth_at(level, g) * now
                    absorbed = term if absorbed is None else absorbed + term
                    later.append(now)
                flux = tuple(later)
                heat = (sunshine - sunshine * albedo_at(level)) * (plain[level] + 2.0 * absorbed)
                at = pl.multiple_of(level * rows, rows)
                low, high = pl.ds(at, half), pl.ds(pl.multiple_of(at + half, half), half)
                start = joined(anomaly_in[low, :], anomaly_in[high, :], group)
                field[pl.ds(half * group * slab + level, half, stride=slab), :] = heat + start
                if group == 0:
                    heat_held[level] = heat
                else:
                    other = heat_held[level]
                    heat_out[low, :] = jnp.where(front, other, heat)
                    heat_out[high, :] = jnp.where(front, heat, other)
            return flux

        lax.fori_loop(0, levels // UNROLL, up, tuple(zero for _ in range(points)))

    def row_levels(row, first):
        return field[pl.ds(places[row] * slab + first, 8), :]

    lane = lax.broadcasted_iota(jnp.int32, (8, lanes), 1)
    lane_row, lane_edge = lane // EDGE, lane % EDGE

    def gather_edges(start, wanted, first):
        value = start
        for place, row in wanted:
            moved = pltpu.roll(row_levels(row, first), (place * EDGE + HALO) % lanes, 1)
            value = jnp.where(lane_row == place, moved, value)
        return value

    blocks = [*range(0, levels - 7, 8)] + ([levels - 8] if levels % 8 else [])
    outer = [(r, r) for r in (*range(HALO), *range(rows - HALO, rows))]
    inner = [(r, r) for r in range(HALO, rows - HALO)]

    def remote(source, target, number, to_tile, to_band):
        return pltpu.make_async_remote_copy(
            src_ref=source, dst_ref=target, send_sem=send_sem.at[number], recv_sem=recv_sem.at[number],
            device_id=(to_tile, to_band), device_id_type=MESH,
        )

    def slabs(first_row):
        return field.at[pl.ds(places[first_row] * slab, HALO * slab)]

    to_north = [remote(slabs(0), slabs(rows), 0, north, band)]
    to_south = [remote(slabs(rows - HALO), slabs(-HALO), 1, south, band)]
    to_side = []
    for j, side in enumerate(sides):
        to_north.append(remote(corner.at[0], got_corner.at[0, j], 2 + 3 * j, north, side))
        to_south.append(remote(corner.at[1], got_corner.at[1, j], 3 + 3 * j, south, side))
        to_side.append(remote(strip, got.at[j], 4 + 3 * j, tile, side))

    anomaly_copy.wait()
    radiate(0)

    def pack_corner(first_row):
        packed = []
        for j, first in enumerate(blocks):
            if j % HALO == 0:
                packed.append(jnp.zeros((8, lanes), F32))
            wanted = [(j % HALO * HALO + i, first_row + i) for i in range(HALO)]
            packed[-1] = gather_edges(packed[-1], wanted, first)
        return packed

    for end, first_row in enumerate((0, rows - HALO)):
        for v, value in enumerate(pack_corner(first_row)):
            corner[end, v] = value

    peers = n_sides + (1 + n_sides) * (has_north.astype(jnp.int32) + has_south.astype(jnp.int32))
    pl.semaphore_wait(barrier, peers)

    @pl.when(has_north)
    def _():
        for copy in to_north:
            copy.start()

    @pl.when(has_south)
    def _():
        for copy in to_south:
            copy.start()

    @pl.when(jnp.logical_not(has_north))
    def _():
        slabs(-HALO)[...] = jnp.zeros((HALO * slab, lanes), F32)
        for j in range(n_sides):
            got_corner[1, j] = jnp.zeros(corner.shape[1:], F32)

    @pl.when(jnp.logical_not(has_south))
    def _():
        slabs(rows)[...] = jnp.zeros((HALO * slab, lanes), F32)
        for j in range(n_sides):
            got_corner[0, j] = jnp.zeros(corner.shape[1:], F32)

    def pack_outer(first):
        strip[pl.ds(first, 8), :] = gather_edges(jnp.zeros((8, lanes), F32), outer, first)

    def pack_inner(first):
        span = pl.ds(first, 8)
        strip[span, :] = gather_edges(strip[span, :], inner, first)

    for first in blocks:
        pack_outer(first)
    radiate(1)
    heat_copy = pltpu.make_async_copy(heat_out, heat_hbm, out_sem.at[0])
    heat_copy.start()
    for first in blocks:
        pack_inner(first)
    for copy in to_side:
        copy.start()

    @pl.when(has_north)
    def _():
        for copy in to_south:
            copy.wait_recv()

    @pl.when(has_south)
    def _():
        for copy in to_north:
            copy.wait_recv()

    keep_north = jnp.where(has_north, 1.0, 0.0).astype(F32)
    keep_south = jnp.where(has_south, 1.0, 0.0).astype(F32)
    full = rows + 2 * HALO

    def sweep_rows(now, sweep):
        later = [None] * full
        for i in range(sweep, full - sweep):
            x = now[i]
            value = (x + pltpu.roll(x, 1, 1)) + (pltpu.roll(x, lanes - 1, 1) + (now[i - 1] + now[i + 1]))
            if i < HALO:
                value = value * keep_north
            if i >= HALO + rows:
                value = value * keep_south
            later[i] = value
        return later

    def diffuse(step, _):
        firsts = [jnp.minimum((step * TOGETHER + b) * 8, levels - 8) for b in range(TOGETHER)]
        state = [[row_levels(i - HALO, first) for i in range(full)] for first in firsts]
        for sweep in range(1, DIFF_STEPS + 1):
            state = [sweep_rows(now, sweep) for now in state]
        for first, now in zip(firsts, state):
            for r in range(rows):
                smooth[pl.ds(r * smooth_step + first, 8), :] = now[HALO + r] * (mixing_rate**DIFF_STEPS)
        return 0

    lax.fori_loop(0, (len(blocks) + TOGETHER - 1) // TOGETHER, diffuse, 0)
    smooth_copy = pltpu.make_async_copy(smooth, smooth_hbm, out_sem.at[1])
    smooth_copy.start()

    mats_copy.wait()
    for copy in to_side:
        copy.wait_recv()

    def pick(ref, *at):
        west = ref[(*at[:-1], 0, at[-1])]
        if n_sides == 1:
            return west
        return jnp.where(lane_edge < HALO, west, ref[(*at[:-1], 1, at[-1])])

    ends = []
    for end, first_row in ((1, -HALO), (0, rows)):
        ends.append([pick(got_corner, end, v) - here for v, here in enumerate(pack_corner(first_row))])
    differ[pl.ds(differ.shape[0] - 8, 8), :] = jnp.zeros((8, 2 * lanes), F32)
    width = HALO * EDGE
    for j, first in enumerate(blocks):
        span = pl.ds(first, 8)
        differ[span, pl.ds(0, lanes)] = pick(got, span) - strip[span, :]
        above, below = (x[j // HALO] for x in ends)
        above = pltpu.roll(above, (lanes - j % HALO * width) % lanes, 1)
        below = pltpu.roll(below, (lanes + width - j % HALO * width) % lanes, 1)
        beyond = jnp.where(lane < width, above, jnp.where(lane < 2 * width, below, 0.0))
        differ[span, pl.ds(lanes, lanes)] = beyond
    rest, total = differ[...], None
    for _ in range(3):
        part = rest.astype(jnp.bfloat16)
        rest = rest - part.astype(F32)
        term = jnp.dot(part, mats[...], preferred_element_type=F32)
        total = term if total is None else total + term
    fix[...] = total * (mixing_rate**DIFF_STEPS)
    fix_copy = pltpu.make_async_copy(fix, fix_hbm, out_sem.at[2])
    fix_copy.start()

    @pl.when(has_north)
    def _():
        for copy in to_north:
            copy.wait_send()

    @pl.when(has_south)
    def _():
        for copy in to_south:
            copy.wait_send()

    for copy in to_side:
        copy.wait_send()
    for copy in (heat_copy, smooth_copy, fix_copy):
        copy.wait()


def finish(
    rows, levels, heat, smooth_in, fix_in, heat_hbm, smooth_hbm, smooth, fix, fixed, ordered, in_sem, sem
):
    lanes = heat.shape[1]
    half = rows // 2
    step = smooth.shape[0] // rows
    loads = [
        pltpu.make_async_copy(smooth_in, smooth, in_sem.at[0]),
        pltpu.make_async_copy(fix_in, fix, in_sem.at[1]),
    ]
    for copy in loads:
        copy.start()
    heat_copy = pltpu.make_async_copy(heat, heat_hbm, sem.at[0])
    heat_copy.start()
    for copy in loads:
        copy.wait()
    lane_row = lax.broadcasted_iota(jnp.int32, (8, lanes), 1) // EDGE
    copies, done = [heat_copy], 0
    for first in [*range(0, levels - 7, 8)] + ([levels - 8] if levels % 8 else []):
        value = fix[pl.ds(first, 8), :]
        for r in range(rows):
            moved = pltpu.roll(jnp.where(lane_row == r, value, 0.0), (2 * lanes - r * EDGE - HALO) % lanes, 1)
            span = pl.ds(r * step + first, 8)
            fixed[span, :] = smooth[span, :] + moved
        if first + 8 - done < CHUNK and first + 8 < levels:
            continue
        for level in range(done, first + 8):
            for part in range(2):
                eight = fixed[pl.ds(part * half * step + level, half, stride=step), :]
                ordered[pl.ds(level * rows + part * half, half), :] = eight
        span = pl.ds(done * rows, (first + 8 - done) * rows)
        copy = pltpu.make_async_copy(ordered.at[span], smooth_hbm.at[span], sem.at[len(copies)])
        copy.start()
        copies.append(copy)
        done = first + 8
    for copy in copies:
        copy.wait()


def per_device(n_tiles, n_band, optical_depth, albedo, insolation, sunlit, point_weight, anomaly):
    rows, levels, points, lanes = optical_depth.shape
    n_sides = 1 if n_band == 2 else 2
    mats = edge_weights(rows)
    slab = (levels + 7) // 8 * 8 + 2

    def by_level(x):
        return jnp.swapaxes(x, 0, 1).reshape(levels * rows, lanes)

    shape = jax.ShapeDtypeStruct((levels * rows, lanes), F32)
    hbm = pl.BlockSpec(memory_space=pltpu.HBM)
    n_copies = 2 + 3 * n_sides
    deep = (levels + 7) // 8 * 8
    heat, smooth, fix = pl.pallas_call(
        functools.partial(kernel, n_tiles, n_band, rows, levels, points),
        out_shape=(
            shape,
            jax.ShapeDtypeStruct((rows * (slab - 1), lanes), F32),
            jax.ShapeDtypeStruct((deep, lanes), F32),
        ),
        in_specs=[hbm] * 7,
        out_specs=(hbm, hbm, hbm),
        scratch_shapes=[
            pltpu.VMEM((rows * levels * points, lanes), jnp.bfloat16),
            pltpu.VMEM((levels * rows, lanes), jnp.bfloat16),
            pltpu.VMEM((levels * rows, lanes), F32),
            pltpu.VMEM(mats.shape[1:], jnp.bfloat16),
            pltpu.VMEM((rows, lanes), jnp.bfloat16),
            pltpu.SMEM((1, rows), jnp.int32),
            pltpu.SMEM((points,), F32),
            pltpu.VMEM((8 * (levels * points + 1), lanes), F32),
            pltpu.VMEM((levels, points, 8, lanes), F32),
            pltpu.VMEM((levels, points, 8, lanes), F32),
            pltpu.VMEM((levels, 8, lanes), F32),
            pltpu.VMEM((levels, 8, lanes), F32),
            pltpu.VMEM((levels * rows, lanes), F32),
            pltpu.VMEM((rows * (slab - 1), lanes), F32),
            pltpu.VMEM((deep, lanes), F32),
            pltpu.VMEM(((rows + 2 * HALO) * slab, lanes), F32),
            pltpu.VMEM((levels, lanes), F32),
            pltpu.VMEM((2, deep // 32, 8, lanes), F32),
            pltpu.VMEM((n_sides, levels, lanes), F32),
            pltpu.VMEM((2, n_sides, deep // 32, 8, lanes), F32),
            pltpu.VMEM((deep, 2 * lanes), F32),
            pltpu.SemaphoreType.DMA((12,)),
            pltpu.SemaphoreType.DMA((3,)),
            pltpu.SemaphoreType.DMA((n_copies,)),
            pltpu.SemaphoreType.DMA((n_copies,)),
        ],
        compiler_params=pltpu.CompilerParams(
            collective_id=0, has_side_effects=True, vmem_limit_bytes=56 * 1024 * 1024
        ),
    )(
        optical_depth.reshape(rows * levels * points, lanes),
        by_level(albedo), by_level(anomaly), jnp.asarray(mats), insolation, sunlit.T, point_weight,
    )
    heating, smoothed = pl.pallas_call(
        functools.partial(finish, rows, levels),
        out_shape=(shape, shape),
        in_specs=[hbm] * 3,
        out_specs=(hbm, hbm),
        scratch_shapes=[
            pltpu.VMEM((rows * (slab - 1), lanes), F32),
            pltpu.VMEM((deep, lanes), F32),
            pltpu.VMEM((rows * (slab - 1), lanes), F32),
            pltpu.VMEM((levels * rows, lanes), F32),
            pltpu.SemaphoreType.DMA((2,)),
            pltpu.SemaphoreType.DMA((2 + levels // CHUNK + 1,)),
        ],
        compiler_params=pltpu.CompilerParams(vmem_limit_bytes=56 * 1024 * 1024),
    )(heat, smooth, fix)
    return tuple(jnp.swapaxes(x.reshape(levels, rows, lanes), 0, 1) for x in (heating, smoothed))


def solution(mesh):
    placed = (
        P("tiles", None, None, "band"),
        P("tiles", None, "band"),
        P("tiles", "band"),
        P("tiles", "band"),
        P(),
        P("tiles", None, "band"),
    )
    return jax.shard_map(
        functools.partial(per_device, mesh.shape["tiles"], mesh.shape["band"]),
        mesh=mesh,
        in_specs=placed,
        out_specs=(P("tiles", None, "band"), P("tiles", None, "band")),
        check_vma=False,
    )
```
